128 devices in a mesh: dp: 32 (over x, y_lo, z), shard: 4 (over y_hi, core).
Axes of the slice: x: 4, y: 4 (y_hi: 2, y_lo: 2; y = y_hi * 2 + y_lo), z: 4, core: 2. Of those that a mesh axis runs over, the one named last changes fastest.
Arguments:
- tokens: bfloat16 [32768, 768], P(('dp', 'shard')), may hold values from -6 to 6
- bounds: int32 [32, 2], P('dp'), may hold values from 0 to 1024, as said below
- routes: int32 [32768, 2], P(('dp', 'shard')), may hold values from 0 to 63, all different within a row; in each aligned block of 256 rows (0 to 255, 256 to 511, ...) at most 16 rows name the same one
- ln1_gain: bfloat16 [768], P(('dp', 'shard')), may hold values from 0.099609375 to 1.8984375
- ln1_bias: bfloat16 [768], P(('dp', 'shard')), may hold values from -1.5 to 1.5
- query_weight: bfloat16 [768, 768], P(('dp', 'shard')), may hold values from -0.21875 to 0.21875
- key_weight: bfloat16 [768, 768], P(('dp', 'shard')), may hold values from -0.21875 to 0.21875
- value_weight: bfloat16 [768, 768], P(('dp', 'shard')), may hold values from -0.21875 to 0.21875
- output_weight: bfloat16 [768, 768], P(('dp', 'shard')), may hold values from -1.75 to 1.75
- ln2_gain: bfloat16 [768], P(('dp', 'shard')), may hold values from 0.099609375 to 1.8984375
- ln2_bias: bfloat16 [768], P(('dp', 'shard')), may hold values from -1.5 to 1.5
- gate_new: bfloat16 [768, 32], P(('dp', 'shard')), may hold values from -0.15625 to 0.15625
- gate_frozen: bfloat16 [768, 32], P(('dp', 'shard')), may hold values from -0.15625 to 0.15625
- new_in: bfloat16 [32, 768, 3072], P('dp', None, 'shard'), may hold values from -0.21875 to 0.21875
- new_out: bfloat16 [32, 3072, 768], P('dp', 'shard'), may hold values from -0.109375 to 0.109375
- frozen_in: bfloat16 [32, 768, 3072], P('dp', None, 'shard'), may hold values from -0.21875 to 0.21875
- frozen_out: bfloat16 [32, 3072, 768], P('dp', 'shard'), may hold values from -0.109375 to 0.109375
- cotangent: bfloat16 [32768, 768], P(('dp', 'shard')), may hold values from -6 to 6
Outputs:
- layer_out: bfloat16 [32768, 768], P(('dp', 'shard'))
- grad_tokens: bfloat16 [32768, 768], P(('dp', 'shard'))
- grad_query: float32 [768, 768], P(('dp', 'shard'))
- grad_key: float32 [768, 768], P(('dp', 'shard'))
- grad_value: float32 [768, 768], P(('dp', 'shard'))
- grad_output: float32 [768, 768], P(('dp', 'shard'))
- grad_ln1_gain: float32 [768], P(('dp', 'shard'))
- grad_ln1_bias: float32 [768], P(('dp', 'shard'))
- grad_ln2_gain: float32 [768], P(('dp', 'shard'))
- grad_ln2_bias: float32 [768], P(('dp', 'shard'))
- grad_gate_new: float32 [768, 32], P(('dp', 'shard'))
- grad_new_in: float32 [32, 768, 3072], P('dp', None, 'shard')
- grad_new_out: float32 [32, 3072, 768], P('dp', 'shard')
The draws below stay inside these ranges and needn't reach their ends.
Inputs may be any that keep to these rules, and one draw needn't show every extreme that they name: `bounds`: for each group the first boundary is below 256 and the second above 768, so the middle document begins on the group's first device and ends on its last; in one group the boundaries are 0 and 1024. `routes`: each token names two different experts; among the 256 tokens of one device no expert is named more than 16 times, a bound that some block reaches.
All inputs are finite; a program needn't handle non-finite values.
Results may differ from the reference program's by a relative error of at most 0.02.
Values may be sent and summed in bfloat16 or wider, within the bound.
No kernel may reach another device: no remote copies, remote signals or barrier semaphores. Data moves between devices by JAX's collectives and lax.ppermute only.
A program may use at most 192 MiB of HBM per device.

```python
import math
import jax
import jax.numpy as jnp
import numpy as np
from jax import lax

D = 768
FF = 3072
HEADS = 12
HEAD_DIM = 64
TOK_DEV = 256
GROUP = 1024
CAP = 16
TOKENS = 32768
N_DP = 32
N_SHARD = 4


def draw_bounds(key, part):
    key = jax.random.fold_in(key, 11)
    key_start, key_end, key_whole = jax.random.split(key, 3)
    doc_start = jax.random.randint(key_start, (N_DP,), 0, TOK_DEV)
    doc_end = GROUP - jax.random.randint(key_end, (N_DP,), 0, TOK_DEV)
    whole_group = jax.random.randint(key_whole, (), 0, N_DP)
    selected = jnp.arange(N_DP) == whole_group
    doc_start = jnp.where(selected, 0, doc_start)
    doc_end = jnp.where(selected, GROUP, doc_end)
    return jnp.stack([doc_start, doc_end], 1).astype(jnp.int32)


def block_levels(rng, shape, cuts, smallest, largest):
    loudness = 1.0
    for dim, shards_of in cuts:
        draws = jax.random.uniform(jax.random.fold_in(jax.random.fold_in(rng, 6), dim), (shards_of,), jnp.float32, smallest / len(cuts), largest / len(cuts))
        loudness = loudness * jnp.repeat(jnp.exp(draws), shape[dim] // shards_of).reshape((-1,) + (1,) * (len(shape) - 1 - dim))
    return loudness


def assign_block(own_key, own, number, rows, count, top, limit, slope):
    ranking = jax.random.permutation(own_key, count)
    heavy_load, ordinary = load_shares(count, rows * top, limit, slope, True), load_shares(count, rows * top, limit, slope, False)
    places = jnp.arange(count)

    def named(lengths, offset_by):
        used = int((lengths > 0).sum())
        fixed = max(1, used // 4)
        passed = fixed + (places - fixed + offset_by * (used - fixed)) % max(1, count - fixed)
        return jnp.zeros((count,), jnp.int32).at[ranking[jnp.where(places < fixed, places, passed)]].set(jnp.asarray(lengths, jnp.int32))

    lengths = jnp.where(number % 4 == 0, named(heavy_load, number // 4), named(ordinary, number - number // 4 - 1))
    mixed = jax.random.permutation(jax.random.fold_in(own, 3), count)
    donor, sink = mixed[0:count // 2 * 2:2], mixed[1:count // 2 * 2:2]
    room = jnp.minimum(lengths[donor] - 1, limit - lengths[sink]) // 2
    room = jnp.where((donor == ranking[0]) | (sink == ranking[0]) | (lengths[sink] == 0), 0, jnp.maximum(room, 0))
    passed = jax.random.randint(jax.random.fold_in(own, 4), (count // 2,), 0, 1 << 20) % (room + 1)
    lengths = lengths.at[donor].add(-passed).at[sink].add(passed)
    items = jnp.searchsorted(jnp.cumsum(lengths), jnp.arange(rows * top), side="right").astype(jnp.int32)
    table = items.reshape(top, rows).T
    table = table[jax.random.permutation(jax.random.fold_in(own, 1), rows)]
    offset_by = jax.random.randint(jax.random.fold_in(own, 2), (rows, 1), 0, top)
    return jnp.take_along_axis(table, (jnp.arange(top)[None, :] + offset_by) % top, axis=1)


def load_shares(amount, total, bound, lean, full):
    weights = [(1 << 20) // math.isqrt(rank ** lean) + 1 for rank in range(1, amount + 1)]
    largest = bound if full else min(bound, max(-(-total // amount), total * weights[0] // sum(weights)))
    least = 1 if total - largest >= amount - 1 else 0
    counts, rest = [largest] + [least] * (amount - 1), total - largest - least * (amount - 1)
    while rest > 0:
        free = [i for i in range(1, amount) if counts[i] < largest] or [i for i in range(1, amount) if counts[i] < bound]
        pool, left = sum([weights[i] for i in free]), rest
        for i in free:
            addition = min(bound - counts[i], max(1, left * weights[i] // pool), rest)
            counts[i] = counts[i] + addition
            rest = rest - addition
    return np.array(counts)


def noise(own_key, shape, deviation, bound, shards=(), dtype=jnp.bfloat16):
    entries = jax.random.normal(own_key, shape, jnp.float32) * deviation
    if len(shards) > 0:
        entries = block_levels(own_key, shape, shards, -0.22, 0.18) * entries
    return jnp.clip(entries, min=-bound, max=bound).astype(dtype)


def setup_inputs(seed: int = 0) -> dict:
    arg_keys = jax.random.split(jax.random.key(seed), 19)
    tokens = noise(arg_keys[0], (TOKENS, D), 1.0, 6.0, ((0, 128),))
    bounds = draw_bounds(jax.random.fold_in(arg_keys[18], 71), 0)
    routes_keys = jax.random.split(jax.random.fold_in(arg_keys[2], 1), TOKENS // TOK_DEV)
    routes_turns = jax.random.permutation(jax.random.fold_in(arg_keys[2], 3), TOKENS // TOK_DEV)
    routes = jax.vmap(lambda own, number: assign_block(jax.random.fold_in(arg_keys[2], 2), own, number, TOK_DEV, 2 * N_DP, 2, CAP, 2))(routes_keys, routes_turns).reshape((TOKENS, 2))
    ln1_gain = jnp.clip(1.0 + 0.18 * jax.random.normal(arg_keys[3], (D,), jnp.float32), 0.099609375, 1.8984375).astype(jnp.bfloat16)
    ln1_bias = noise(arg_keys[4], (D,), 0.3, 1.5, ((0, 128),))
    query_weight = noise(arg_keys[5], (D, D), D ** -0.5, 0.21875, ((0, 128),))
    key_weight = noise(arg_keys[6], (D, D), D ** -0.5, 0.21875, ((0, 128),))
    value_weight = noise(arg_keys[7], (D, D), D ** -0.5, 0.21875, ((0, 128),))
    output_weight = noise(arg_keys[8], (D, D), (D // 64) ** -0.5, 1.75, ((0, 128),))
    ln2_gain = jnp.clip(1.0 + 0.18 * jax.random.normal(arg_keys[9], (D,), jnp.float32), 0.099609375, 1.8984375).astype(jnp.bfloat16)
    ln2_bias = noise(arg_keys[10], (D,), 0.3, 1.5, ((0, 128),))
    gate_new = noise(arg_keys[11], (D, N_DP), (2 * D) ** -0.5, 0.15625, ((0, 128),))
    gate_frozen = noise(arg_keys[12], (D, N_DP), (2 * D) ** -0.5, 0.15625, ((0, 128),))
    new_in = noise(arg_keys[13], (N_DP, D, FF), D ** -0.5, 0.21875, ((0, 32), (2, 4)))
    new_out = noise(arg_keys[14], (N_DP, FF, D), FF ** -0.5, 0.109375, ((0, 32), (1, 4)))
    frozen_in = noise(arg_keys[15], (N_DP, D, FF), D ** -0.5, 0.21875, ((0, 32), (2, 4)))
    frozen_out = noise(arg_keys[16], (N_DP, FF, D), FF ** -0.5, 0.109375, ((0, 32), (1, 4)))
    cotangent = noise(arg_keys[17], (TOKENS, D), 1.0, 6.0, ((0, 128),))
    return dict(tokens=tokens, bounds=bounds, routes=routes, ln1_gain=ln1_gain, ln1_bias=ln1_bias, query_weight=query_weight, key_weight=key_weight, value_weight=value_weight, output_weight=output_weight, ln2_gain=ln2_gain, ln2_bias=ln2_bias, gate_new=gate_new, gate_frozen=gate_frozen, new_in=new_in, new_out=new_out, frozen_in=frozen_in, frozen_out=frozen_out, cotangent=cotangent)


@jax.custom_vjp
def low(v):
    return lax.optimization_barrier(v.astype(jnp.bfloat16)).astype(jnp.float32)

@jax.custom_vjp
def low_back(v):
    return v

def low_keep(v):
    return (low(v), None)

def low_pass(kept, grad):
    return (grad,)

def back_keep(v):
    return (v, None)

def back_low(kept, grad):
    return (low(grad),)
low.defvjp(low_keep, low_pass)
low_back.defvjp(back_keep, back_low)

def matmul(left, right):
    return jnp.dot(left, right, precision=lax.Precision.HIGHEST, preferred_element_type=jnp.float32)

def layer_norm(values_in):
    center = values_in - lax.optimization_barrier(jnp.mean(values_in, -1, keepdims=True))
    return center * lax.rsqrt(lax.optimization_barrier(jnp.mean(center * center, -1, keepdims=True)) + 1e-05)

def group_attention(inputs):
    queries, keys_in, values_in, segment = inputs
    positions = jnp.arange(queries.shape[0])
    scores = jnp.einsum('qhd,khd->hqk', queries, keys_in, precision=lax.Precision.HIGHEST) * HEAD_DIM ** (-0.5)
    scores = low_back(scores)
    allowed = (segment[:, None] == segment[None, :]) & (positions[None, :] <= positions[:, None])
    scores = jnp.where(allowed[None], scores, -1e+30)
    highest = lax.optimization_barrier(jnp.max(scores, -1, keepdims=True))
    exponent = jnp.exp(scores - highest)
    attn_prob = exponent / lax.optimization_barrier(jnp.sum(exponent, -1, keepdims=True))
    return jnp.einsum('hqk,khd->qhd', low(attn_prob), values_in, precision=lax.Precision.HIGHEST)

def expert_apply(inputs):
    rows_in, weight_in, weight_out = inputs
    pre_act = low_back(matmul(rows_in, weight_in))
    hidden = low(jax.nn.gelu(pre_act, approximate=True))
    return low_back(low(matmul(hidden, weight_out)))

def reference(tokens, bounds, routes, ln1_gain, ln1_bias, query_weight, key_weight, value_weight, output_weight, ln2_gain, ln2_bias, gate_new, gate_frozen, new_in, new_out, frozen_in, frozen_out, cotangent):
    devices = N_DP * N_SHARD
    positions = jnp.arange(GROUP).astype(jnp.int32)
    segment = (positions[None, :] >= bounds[:, 0:1]).astype(jnp.int32) + (positions[None, :] >= bounds[:, 1:2]).astype(jnp.int32)
    dev_routes = routes.reshape(devices, 2 * TOK_DEV)
    onehot = (dev_routes[:, :, None] == jnp.arange(2 * N_DP).astype(jnp.int32)[None, None, :]).astype(jnp.int32)
    earlier = jnp.cumsum(onehot, 1).astype(jnp.int32) - onehot
    slot_pos = lax.optimization_barrier(jnp.sum(earlier * onehot, -1)).astype(jnp.int32).reshape(TOKENS, 2)
    device_of = (jnp.arange(TOKENS) // TOK_DEV).astype(jnp.int32)
    gslot = (device_of[:, None] * CAP + slot_pos).astype(jnp.int32)
    gate_old = gate_frozen.astype(jnp.float32)
    old_in = frozen_in.astype(jnp.float32)
    old_out = frozen_out.astype(jnp.float32)
    head_shape = (N_DP, GROUP, HEADS, HEAD_DIM)

    def forward(x_in, gain_one, bias_one, w_query, w_key, w_value, w_output, gain_two, bias_two, gate_mine, win_new, wout_new):
        normed_one = low(layer_norm(x_in) * gain_one + bias_one)
        queries = low_back(low(matmul(normed_one, w_query)))
        keys_all = low_back(low(matmul(normed_one, w_key)))
        values_all = low_back(low(matmul(normed_one, w_value)))
        attended = lax.map(jax.checkpoint(group_attention), (queries.reshape(head_shape), keys_all.reshape(head_shape), values_all.reshape(head_shape), segment))
        attended = low_back(low(attended.reshape(TOKENS, D)))
        resid = x_in + low_back(matmul(attended, w_output))
        normed_two = low(layer_norm(resid) * gain_two + bias_two)
        logits = low_back(matmul(normed_two, jnp.concatenate([gate_mine, gate_old], 1)))
        chosen = jnp.take_along_axis(logits, routes, 1)
        highest = lax.optimization_barrier(jnp.max(chosen, -1, keepdims=True))
        exponent = jnp.exp(chosen - highest)
        combine = exponent / lax.optimization_barrier(jnp.sum(exponent, -1, keepdims=True))
        spread = jnp.broadcast_to(normed_two[:, None, :], (TOKENS, 2, D))
        buffer = jnp.zeros((2 * N_DP, devices * CAP, D), jnp.float32).at[routes, gslot].set(spread)
        buffer = low_back(buffer)
        weights_in = jnp.concatenate([win_new, old_in], 0)
        weights_out = jnp.concatenate([wout_new, old_out], 0)
        outputs = lax.map(jax.checkpoint(expert_apply), (buffer, weights_in, weights_out))
        picked = outputs[routes, gslot]
        return resid + lax.optimization_barrier(jnp.sum(combine[:, :, None] * picked, 1))
    primals = (tokens, ln1_gain, ln1_bias, query_weight, key_weight, value_weight, output_weight, ln2_gain, ln2_bias, gate_new, new_in, new_out)
    primals = tuple((item.astype(jnp.float32) for item in primals))
    result, pull = jax.vjp(forward, *primals)
    grads = pull(cotangent.astype(jnp.float32))
    return (result.astype(jnp.bfloat16), grads[0].astype(jnp.bfloat16), grads[3], grads[4], grads[5], grads[6], grads[1], grads[2], grads[7], grads[8], grads[9], grads[10], grads[11])
```

```python
import functools

import jax
import jax.numpy as jnp
from jax import lax
from jax.experimental import pallas as pl
from jax.experimental.pallas import tpu as pltpu
from jax.sharding import PartitionSpec as P

HEAD_DIM = 64
BOTH = ("dp", "shard")
F32 = jnp.float32
BF16 = jnp.bfloat16
I32 = jnp.int32
VMEM_BYTES = 56 * 2**20
PAD = 8
SMEM = pltpu.SMEM
VMEM = pltpu.VMEM


def mul(left, right):
    return jnp.dot(left, right, preferred_element_type=F32)


def contract_rows(left, right):
    return lax.dot_general(left, right, (((0,), (0,)), ((), ())), preferred_element_type=F32)


def contract_cols(left, right):
    return lax.dot_general(left, right, (((1,), (1,)), ((), ())), preferred_element_type=F32)


def iota(shape, dim):
    return lax.broadcasted_iota(I32, shape, dim)


def norm_stats(values_in):
    center = values_in - jnp.mean(values_in, -1, keepdims=True)
    scaling = lax.rsqrt(jnp.mean(center * center, -1, keepdims=True) + 1e-05)
    return (center * scaling, scaling)


def norm_back(grad_normed, normed, scaling):
    mean_grad = jnp.mean(grad_normed, -1, keepdims=True)
    mean_cross = jnp.mean(grad_normed * normed, -1, keepdims=True)
    return scaling * (grad_normed - mean_grad - normed * mean_cross)


def in_three(values_in):
    first = values_in.astype(BF16).astype(F32)
    rest = values_in - first
    second = rest.astype(BF16).astype(F32)
    return first, second, rest - second


def in_lanes(terms, rows):
    lane = iota((rows, 128), 1)
    out = jnp.zeros((rows, 128), F32)
    for k, term in enumerate(terms):
        out = jnp.where(lane == k, term, out)
    return out


def spread(held, width, rows_first):
    padded = width // held * PAD
    shape, row_dim = ((width, padded), 0) if rows_first else ((padded, width), 1)
    row, col = iota(shape, row_dim), iota(shape, 1 - row_dim)
    block = block_of(row, held)
    return (col == block * PAD + (row - block * held)).astype(F32).astype(BF16)


def block_of(row, held):
    step = -(-(1 << 16) // held)
    return lax.shift_right_logical(row * step, 16)


def vector_rows(lanes, held, width, which, first=0):
    row = iota((lanes.shape[1], width), 1)
    lane = iota((lanes.shape[1], width), 0) - first
    pick = (lane == row - block_of(row, held) * held).astype(F32)
    wide = mul(lanes, pick.astype(BF16))
    col = iota(wide.shape, 1)
    wanted = iota(wide.shape, 0) == block_of(col, held) * PAD + which
    return jnp.sum(jnp.where(wanted, wide, 0.0), 0, keepdims=True)


def call(body, out_shapes, args, **more):
    return pl.pallas_call(
        body,
        out_shape=out_shapes,
        compiler_params=pltpu.CompilerParams(vmem_limit_bytes=VMEM_BYTES),
        cost_estimate=pl.CostEstimate(flops=1, bytes_accessed=1, transcendentals=1),
        **more,
    )(*args)


tie = lax.optimization_barrier


def shaped(shape, dtype):
    return jax.ShapeDtypeStruct(shape, dtype)


def pack_body(part, in_wide, query_ref, key_ref, value_ref, out_ref, new_ref, old_ref, *refs):
    (gain_one, bias_one, gain_two, bias_two), blocks_ref, work_ref = refs[:4], refs[4], refs[5]
    held, width = out_ref.shape
    half, gates, at = width // 2, new_ref.shape[1], 3 * part
    work_ref[...] = jnp.zeros_like(work_ref)
    for k in range(work_ref.shape[0]):
        for m, ref in enumerate((query_ref, key_ref, value_ref)):
            piece = ref[:, k * part : (k + 1) * part]
            work_ref[k, :held, m * part : (m + 1) * part] = piece.astype(F32)
        work_ref[k, :held, at : at + gates] = new_ref[...].astype(F32)
        work_ref[k, :held, at + gates : at + 2 * gates] = old_ref[...].astype(F32)
        side = out_ref[:, k % 2 * half : (k % 2 + 1) * half]
        work_ref[k, :held, in_wide : in_wide + half] = side.astype(F32)
        work_ref[k, held : held + 1, :held] = gain_one[...].astype(F32)
        work_ref[k, held + 1 : held + 2, :held] = bias_one[...].astype(F32)
        work_ref[k, held : held + 1, at : at + held] = gain_two[...].astype(F32)
        work_ref[k, held + 1 : held + 2, at : at + held] = bias_two[...].astype(F32)
    blocks = work_ref[...].astype(BF16)

    def put(k, carry):
        blocks_ref[k] = blocks
        return carry

    lax.fori_loop(0, blocks_ref.shape[0], put, 0)


def slots_body(n_dp, capacity, routes_ref, routes_t_ref, cols_ref, lines_ref):
    rows = routes_ref.shape[0]
    routes = routes_ref[...]
    hot = [
        (iota((rows, 2 * n_dp), 1) == routes[:, k : k + 1]).astype(F32) for k in range(2)
    ]
    earlier = (iota((rows, rows), 1) < iota((rows, rows), 0)).astype(F32).astype(BF16)
    count = mul(earlier, (hot[0] + hot[1]).astype(BF16))
    expert = routes
    base = jnp.where(expert < n_dp, 2 * expert, 2 * expert - 2 * n_dp + 1) * capacity
    cols = [
        base[:, k : k + 1] + jnp.sum(count * hot[k], 1, keepdims=True).astype(I32)
        for k in range(2)
    ]
    lane = iota(cols_ref.shape, 1)
    cols_ref[...] = jnp.where(lane == 0, cols[0], cols[1])
    routes_t = routes_t_ref[...]
    hot_t = [
        (iota((2 * n_dp, rows), 0) == routes_t[k : k + 1]).astype(F32) for k in range(2)
    ]
    later = (iota((rows, rows), 0) < iota((rows, rows), 1)).astype(F32).astype(BF16)
    count_t = mul((hot_t[0] + hot_t[1]).astype(BF16), later)
    base_t = jnp.where(routes_t < n_dp, 2 * routes_t, 2 * routes_t - 2 * n_dp + 1) * capacity
    lines = [
        base_t[k : k + 1] + jnp.sum(count_t * hot_t[k], 0, keepdims=True).astype(I32)
        for k in range(2)
    ]
    sub = iota(lines_ref.shape, 0)
    lines_ref[...] = jnp.where(sub == 0, lines[0], lines[1])


def seen_bias(bounds_ref, first, rows, keys, turned=False):
    query = iota((1, rows) if turned else (rows, 1), int(turned)) + first
    key = iota((keys, 1) if turned else (1, keys), 1 - int(turned))
    start, end = bounds_ref[0, 0], bounds_ref[0, 1]

    def doc(pos):
        return (pos >= start).astype(I32) + (pos >= end).astype(I32)

    seen = (doc(query) == doc(key)) & (key <= query)
    return jnp.where(seen, 0.0, -1e30)


def attention_body(held, bounds_ref, shard_ref, got_ref, *refs):
    x_refs, (weight_ref, vector_ref, n_ref, qkv_ref), refs = refs[:4], refs[4:8], refs[8:]
    near_ref, sib_ref, far_ref, att_wide_ref, total_ref = refs
    tile, width = x_refs[0].shape
    part = att_wide_ref.shape[1]
    shard = shard_ref[0, 0]
    got = got_ref[...]
    weight_ref[...] = mul(spread(held, width, True), got).astype(BF16)
    lanes, last = got[:, :128], got[:, got.shape[1] - 128 :]
    first = 3 * part - (got.shape[1] - 128)
    gain = vector_rows(lanes, held, width, held)
    bias = vector_rows(lanes, held, width, held + 1)
    sub = iota(vector_ref.shape, 0)
    vectors = jnp.where(sub == 0, gain, bias)
    vectors = jnp.where(sub == 2, vector_rows(last, held, width, held, first), vectors)
    vector_ref[...] = jnp.where(
        sub == 3, vector_rows(last, held, width, held + 1, first), vectors
    )
    for k, x_ref in enumerate(x_refs):
        at = pl.ds(pl.multiple_of((shard ^ k) * tile, tile), tile)
        normed, unused = norm_stats(x_ref[...].astype(F32))
        n_one = (normed * gain + bias).astype(BF16)
        n_ref[at, :] = n_one
        out = mul(n_one, weight_ref[...])
        scale = jnp.where(iota(out.shape, 1) < part, HEAD_DIM ** (-0.5), 1.0)
        qkv_ref[at, :] = (out.astype(BF16).astype(F32) * scale).astype(BF16)
    for block in range(4):
        first, keys = block * tile, (block + 1) * tile
        hidden = seen_bias(bounds_ref, first, tile, keys)
        totals = []
        for head in range(part // HEAD_DIM):
            at = head * HEAD_DIM
            query = qkv_ref[first:keys, at : at + HEAD_DIM]
            key = qkv_ref[0:keys, part + at : part + at + HEAD_DIM]
            value = qkv_ref[0:keys, 2 * part + at : 2 * part + at + HEAD_DIM]
            scores = contract_cols(query, key) + hidden
            highest = jnp.max(scores, 1, keepdims=True)
            exponent = jnp.exp(scores - highest)
            total = jnp.sum(exponent, 1, keepdims=True)
            prob = (exponent * (1.0 / total)).astype(BF16)
            att_wide_ref[first:keys, at : at + HEAD_DIM] = mul(prob, value)
            totals.append(highest + jnp.log(total))
        total_ref[:, first:keys] = in_lanes(totals, tile).T[: total_ref.shape[0]]
    for k, put in enumerate((near_ref, sib_ref, far_ref.at[:tile], far_ref.at[tile:])):
        at = pl.ds(pl.multiple_of((shard ^ k) * tile, tile), tile)
        put[...] = att_wide_ref[at, :].astype(BF16)


def router_body(
    held,
    n_dp,
    shard_ref,
    x_ref,
    grad_ref,
    near_ref,
    sib_ref,
    far_ref,
    last_ref,
    mine_ref,
    other_ref,
    gates_ref,
    vector_ref,
    routes_ref,
    lines_ref,
    weight_ref,
    resid_ref,
    x_two_ref,
    comb_ref,
    out_ref,
):
    rows, width = x_ref.shape
    slots = out_ref.shape[0]
    part = near_ref.shape[1]
    shard = shard_ref[0, 0]
    first_core = shard % 2 == 0
    left = jnp.where(first_core, mine_ref[...], other_ref[...])
    right = jnp.where(first_core, other_ref[...], mine_ref[...])
    got = jnp.concatenate([left, right], 1)
    weight_ref[...] = mul(spread(held, width, True), got).astype(BF16)
    gain, bias = vector_ref[2:3, :], vector_ref[3:4, :]
    resid = x_ref[...].astype(F32)
    for k, ref in enumerate((near_ref, sib_ref, far_ref.at[:rows], last_ref.at[rows:])):
        at = pl.ds(pl.multiple_of((shard ^ k) * part, part), part)
        resid = resid + mul(ref[...], weight_ref[at, :])
    resid_ref[...] = resid
    normed, unused = norm_stats(resid)
    x_two = (normed * gain + bias).astype(BF16)
    x_two_ref[...] = x_two
    logits = mul(x_two, gates_ref[:, gates_ref.shape[1] - 128 :])
    lane = iota(logits.shape, 1) - (128 - 2 * n_dp)
    chosen = [
        jnp.sum(jnp.where(lane == routes_ref[:, k : k + 1], logits, 0.0), 1, keepdims=True)
        for k in range(2)
    ]
    top = jnp.maximum(chosen[0], chosen[1])
    raw = [jnp.exp(c - top) for c in chosen]
    comb = [r / (raw[0] + raw[1]) for r in raw]
    comb_ref[...] = in_lanes(comb, rows)
    slot = iota((slots, rows), 0)
    place = [(slot == lines_ref[k : k + 1, :]).astype(F32).astype(BF16) for k in range(2)]
    both = (place[0].astype(F32) + place[1].astype(F32)).astype(BF16)
    out_ref[:, :width] = mul(both, x_two).astype(BF16)
    terms = [in_lanes(in_three(c), rows).astype(BF16) for c in comb]
    placed = mul(place[0], terms[0]) + mul(place[1], terms[1])
    out_ref[:, width : width + 128] = placed.astype(BF16)
    out_ref[:, width + 128 :] = mul(both, grad_ref[...]).astype(BF16)


def expert_body(
    shard_ref,
    rows_ref,
    *refs,
):
    own_refs, sib_refs, far_ref = refs[:2], refs[2:4], refs[4]
    back_ref, grad_y_ref, hidden_ref, grad_pre_ref = refs[5:9]
    held_ref, hid_ref, pre_ref, sum_out_ref, sum_back_ref, sems, out_sems = refs[9:]
    slots, width = grad_y_ref.shape
    wide = width + 128
    chunk = 256
    pieces = [slice(k * chunk, (k + 1) * chunk) for k in range(width // chunk)]
    shard = shard_ref[0, 0]
    sources = (
        own_refs,
        [far_ref.at[shard ^ 2, k] for k in range(2)],
        sib_refs,
        [far_ref.at[shard ^ 3, k] for k in range(2)],
    )
    copies = [
        [
            pltpu.make_async_copy(ref, held_ref.at[k, m], sems.at[k, m])
            for m, ref in enumerate(parts)
        ]
        for k, parts in enumerate(sources)
    ]
    for copy in sum(copies, []):
        copy.start()
    comb = jnp.sum(rows_ref[:, width:wide].astype(F32), 1, keepdims=True)
    grad_y_ref[...] = (comb * rows_ref[:, wide:].astype(F32)).astype(BF16)

    def hide(q, at):
        pre = mul(rows_ref[:, :width], held_ref[q, 0, :, at])
        grad_hidden = contract_cols(grad_y_ref[...], held_ref[q, 1, at, :])
        square = pre * pre
        tanh = jnp.tanh(pre * (0.7978845608028654 + 0.035677408136300125 * square))
        share = 0.5 + 0.5 * tanh
        hid = pre * share
        hid_ref[q, :, at] = hid.astype(BF16)
        slope = share + (hid * (1.0 - share)) * (
            1.5957691216057308 + 0.21406444881780074 * square
        )
        pre_ref[q, :, at] = (grad_hidden * slope).astype(BF16)

    def join(q, at):
        out = mul(hid_ref[q], held_ref[q, 1, :, at])
        back = contract_cols(pre_ref[q], held_ref[q, 0, at, :])
        return out, back

    def saves(q):
        at = pl.ds(pl.multiple_of(q * width, width), width)
        return (
            pltpu.make_async_copy(hid_ref.at[q], hidden_ref.at[:, at], out_sems.at[0, q]),
            pltpu.make_async_copy(pre_ref.at[q], grad_pre_ref.at[:, at], out_sems.at[1, q]),
        )

    for copy in copies[0]:
        copy.wait()
    for at in pieces:
        hide(0, at)
    for k, group in enumerate(copies[1:]):
        for copy in group:
            copy.wait()
        for save in saves(k):
            save.start()
        for at in pieces:
            hide(k + 1, at)
            out, back = join(k, at)
            if k == 0:
                sum_out_ref[:, at] = out
                sum_back_ref[:, at] = back
            else:
                sum_out_ref[:, at] += out
                sum_back_ref[:, at] += back
    last = len(copies) - 1
    for save in saves(last):
        save.start()
    dcomb = jnp.zeros((slots, 1), F32)
    for at in pieces:
        out, back = join(last, at)
        out = (sum_out_ref[:, at] + out).astype(BF16)
        back_ref[:, at] = (sum_back_ref[:, at] + back).astype(BF16)
        last_at = slice(wide + at.start, wide + at.stop)
        back_ref[:, last_at] = out
        dcomb += jnp.sum(rows_ref[:, last_at].astype(F32) * out.astype(F32), 1, keepdims=True)
    back_ref[:, width:wide] = in_lanes(in_three(dcomb), slots).astype(BF16)
    for k in range(len(copies)):
        for save in saves(k):
            save.wait()


def expert_call(shard, rows, weights):
    slots = rows.shape[0]
    width = quarter = weights[0].shape[1]
    inside = pl.BlockSpec(memory_space=VMEM)
    anywhere = pl.BlockSpec(memory_space=pl.ANY)
    return call(
        expert_body,
        (
            shaped(rows.shape, BF16),
            shaped((slots, width), BF16),
            shaped((slots, 4 * quarter), BF16),
            shaped((slots, 4 * quarter), BF16),
        ),
        (shard, rows, *weights),
        in_specs=[pl.BlockSpec(memory_space=SMEM), inside] + [anywhere] * len(weights),
        out_specs=[inside] * 2 + [anywhere] * 2,
        scratch_shapes=[
            pltpu.VMEM((4, 2, quarter, quarter), BF16),
            pltpu.VMEM((4, slots, quarter), BF16),
            pltpu.VMEM((4, slots, quarter), BF16),
            pltpu.VMEM((slots, width), F32),
            pltpu.VMEM((slots, width), F32),
            pltpu.SemaphoreType.DMA((4, 2)),
            pltpu.SemaphoreType.DMA((2, 4)),
        ],
    )


def turn_body(rows_ref, grad_y_ref, rows_t_ref, grad_y_t_ref):
    rows_t_ref[...] = rows_ref[:, : rows_t_ref.shape[0]].T
    grad_y_t_ref[...] = grad_y_ref[...].T


def weight_grad_body(rows_t_ref, grad_y_t_ref, hidden_ref, grad_pre_ref, *refs):
    grads = [
        mul(rows_t_ref[...], grad_pre_ref[...]),
        mul(grad_y_t_ref[...], hidden_ref[...]),
    ]
    for k, ref in enumerate(refs[-2:]):
        grad = grads[k] if len(refs) == 2 else grads[k] + refs[k][...].astype(F32)
        ref[...] = grad.astype(ref.dtype)


def weight_grads(rows_t, grad_y_t, hidden, grad_pre, which, dtype, sibs=()):
    width, slots = grad_y_t.shape
    quarter = hidden.shape[1] // 4
    chunk = 256
    pieces = quarter // chunk
    whole = pl.BlockSpec((width, slots), lambda c: (0, 0))
    piece = pl.BlockSpec((slots, chunk), lambda c: (0, which * pieces + c))
    return call(
        weight_grad_body,
        (shaped((width, quarter), dtype),) * 2,
        (rows_t, grad_y_t, hidden, grad_pre, *sibs),
        grid=(pieces,),
        in_specs=[whole] * 2
        + [piece] * 2
        + [pl.BlockSpec((width, chunk), lambda c: (0, c))] * len(sibs),
        out_specs=[pl.BlockSpec((width, chunk), lambda c: (0, c))] * 2,
    )


def new_grads_body(shard_ref, in_ref, out_ref, far_in_ref, far_out_ref, grad_in_ref, grad_out_ref):
    new_here = shard_ref[0, 0] < 2
    grad_in_ref[0] = jnp.where(new_here, in_ref[...], far_in_ref[0].astype(F32))
    grad_out_ref[0] = jnp.where(new_here, out_ref[...], far_out_ref[0].astype(F32)).T


def new_grads_call(shard, own, far_in, far_out):
    quarter = own[0].shape[0]
    tile = quarter // 3
    piece = pl.BlockSpec((quarter, tile), lambda c: (0, c))
    one = pl.BlockSpec((1, quarter, tile), lambda c: (0, 0, c))
    return call(
        new_grads_body,
        (shaped((1, quarter, quarter), F32),) * 2,
        (shard, *own, far_in, far_out),
        grid=(3,),
        in_specs=[pl.BlockSpec(memory_space=SMEM), piece, piece, one, one],
        out_specs=[one, pl.BlockSpec((1, tile, quarter), lambda c: (0, c, 0))],
    )


def token_back_body(
    held,
    n_dp,
    back_ref,
    cols_ref,
    routes_ref,
    comb_ref,
    grad_ref,
    resid_ref,
    x_two_ref,
    gates_ref,
    vector_ref,
    resid_grad_ref,
    att_ref,
    gate_ref,
):
    rows, width = grad_ref.shape
    slots = back_ref.shape[0]
    slot = iota((rows, slots), 1)
    back = [
        mul(
            (slot == cols_ref[:, k : k + 1]).astype(F32).astype(BF16),
            back_ref[:, : width + 128],
        )
        for k in range(2)
    ]
    dcomb = [jnp.sum(b[:, width:], 1, keepdims=True) for b in back]
    comb = [comb_ref[:, k : k + 1] for k in range(2)]
    mean = comb[0] * dcomb[0] + comb[1] * dcomb[1]
    dlog = [c * (d - mean) for c, d in zip(comb, dcomb)]
    lane = iota((rows, 128), 1) - (128 - 2 * n_dp)
    dlogits = jnp.where(lane == routes_ref[:, 0:1], dlog[0], 0.0)
    dlogits = jnp.where(lane == routes_ref[:, 1:2], dlog[1], dlogits).astype(BF16)
    gate = gates_ref[:, gates_ref.shape[1] - 128 :]
    grad_x_two = contract_cols(dlogits, gate) + back[0][:, :width] + back[1][:, :width]
    normed, scaling = norm_stats(resid_ref[...])
    sums = [jnp.sum(grad_x_two * normed, 0, keepdims=True), jnp.sum(grad_x_two, 0, keepdims=True)]
    gain = vector_ref[2:3, :]
    grad_resid = grad_ref[...].astype(F32) + norm_back(grad_x_two * gain, normed, scaling)
    resid_grad_ref[...] = grad_resid
    att_ref[...] = grad_resid.astype(BF16)
    spread_all = spread(held, width, False)
    turned = contract_cols(spread_all, x_two_ref[...]).astype(BF16)
    own_gates = jnp.where(lane < n_dp, dlogits.astype(F32), 0.0).astype(BF16)
    last = 128 - 2 * n_dp + n_dp
    gate_ref[...] = mul(turned, own_gates) + sums_in_lanes(spread_all, sums, last)


def sums_in_lanes(spread_all, sums, first):
    sub = iota((128, sums[0].shape[1]), 0)
    lines = jnp.zeros(sub.shape, F32)
    for k, row in enumerate(sums):
        high, low, unused = in_three(row)
        lines = jnp.where(sub == first + 2 * k, high, lines)
        lines = jnp.where(sub == first + 2 * k + 1, low, lines)
    return contract_cols(spread_all, lines.astype(BF16))


def projection_back_body(
    held,
    shard_ref,
    att_ref,
    weight_ref,
    near_ref,
    sib_ref,
    far_ref,
    far_sib_ref,
    grad_ref,
    *refs,
):
    out_refs, all_ref, owned_ref = refs[:4], *refs[4:]
    tile, width = near_ref.shape
    part = att_ref.shape[1]
    shard = shard_ref[0, 0]
    for k, ref in enumerate((near_ref, sib_ref, far_ref, far_sib_ref)):
        at = pl.ds(pl.multiple_of((shard ^ k) * tile, tile), tile)
        all_ref[at, :] = ref[...]
    mine = pl.ds(pl.multiple_of(shard * part, part), part)
    grad_ref[...] = contract_cols(all_ref[...], weight_ref[mine, :]).astype(BF16)
    turned = contract_cols(spread(held, part, False), att_ref[...].astype(BF16)).astype(BF16)
    owned = mul(turned, all_ref[...]).astype(BF16)
    extent = owned.shape[0]
    for k in range(width // part):
        owned_ref[k * extent : (k + 1) * extent, :] = owned[:, k * part : (k + 1) * part]
    for k, out_ref in enumerate(out_refs):
        at = pl.ds(pl.multiple_of((shard ^ k) * extent, extent), extent)
        out_ref[...] = owned_ref[at, :]


def assemble_body(shard_ref, all_ref, near_ref, sib_ref, far_ref, last_ref, out_ref):
    rows, part = near_ref.shape
    shard = shard_ref[0, 0]
    step = pl.program_id(0)
    for k, ref in enumerate((near_ref, sib_ref, far_ref, last_ref)):
        at = pl.ds(pl.multiple_of((shard ^ k) * rows, rows), rows)

        @pl.when(step == 0)
        def _(at=at, ref=ref):
            out_ref[at, :] = ref[:, :128]

        @pl.when(step == 1)
        def _(at=at, ref=ref):
            out_ref[at, : part - 128] = ref[:, 128:]
            out_ref[at, part - 128 :] = jnp.zeros((rows, 256 - part), BF16)


def attention_back_body(
    held,
    bounds_ref,
    shard_ref,
    n_ref,
    qkv_ref,
    att_ref,
    total_ref,
    weight_ref,
    gate_ref,
    grad_ref,
    *refs,
):
    x_refs, owned_ref, part_refs = refs[:4], refs[4], refs[5:9]
    grads_ref, key_ref, value_ref = refs[9:]
    tile, width = x_refs[0].shape
    part = att_ref.shape[1]
    shard = shard_ref[0, 0]
    key_ref[...] = jnp.zeros_like(key_ref)
    value_ref[...] = jnp.zeros_like(value_ref)
    heads = part // HEAD_DIM
    for block in range(4):
        first, keys = block * tile, (block + 1) * tile
        hidden = seen_bias(bounds_ref, first, tile, keys, True)
        product = grad_ref[first:keys, :].astype(F32) * att_ref[first:keys, :]
        deltas = [
            jnp.sum(product[:, k * HEAD_DIM : (k + 1) * HEAD_DIM], 1, keepdims=True)
            for k in range(heads)
        ]
        deltas = in_lanes(deltas, tile).T
        queries = []
        for head in range(heads):
            at = head * HEAD_DIM
            mine = slice(at, at + HEAD_DIM)
            query = qkv_ref[first:keys, mine]
            key = qkv_ref[0:keys, part + at : part + at + HEAD_DIM]
            value = qkv_ref[0:keys, 2 * part + at : 2 * part + at + HEAD_DIM]
            grad = grad_ref[first:keys, mine]
            scores = contract_cols(key, query) + hidden
            prob = jnp.exp(scores - total_ref[head : head + 1, first:keys])
            grad_prob = contract_cols(value, grad)
            grad_score = (prob * (grad_prob - deltas[head : head + 1])).astype(BF16)
            queries.append(contract_rows(key, grad_score) * HEAD_DIM ** (-0.5))
            key_ref[0:keys, mine] += mul(grad_score, query)
            value_ref[0:keys, mine] += mul(prob.astype(BF16), grad)
        grads_ref[first:keys, :part] = jnp.concatenate(queries, 0).T.astype(BF16)
    grads_ref[:, part : 2 * part] = key_ref[...].astype(BF16)
    grads_ref[:, 2 * part :] = value_ref[...].astype(BF16)
    sums = [jnp.zeros((1, width), F32)] * 2
    for k, (x_ref, part_ref) in enumerate(zip(x_refs, part_refs)):
        at = pl.ds(pl.multiple_of((shard ^ k) * tile, tile), tile)
        grad_n = contract_cols(grads_ref[at, :], weight_ref[:, : 3 * part])
        part_ref[...] = grad_n.astype(BF16)
        normed, unused = norm_stats(x_ref[...].astype(F32))
        sums[0] += jnp.sum(grad_n * normed, 0, keepdims=True)
        sums[1] += jnp.sum(grad_n, 0, keepdims=True)
    spread_all = spread(held, width, False)
    wide = 3 * part
    owned = jnp.zeros((spread_all.shape[0], wide), F32)
    for block in range(4):
        at = slice(block * tile, (block + 1) * tile)
        turned = contract_cols(spread_all, n_ref[at, :]).astype(BF16)
        owned += mul(turned, grads_ref[at, :])
    start = -(-wide // 128) * 128 - 128
    owned_ref[:, :start] = owned[:, :start].astype(BF16)
    low = jnp.pad(owned[:, start:], ((0, 0), (0, start + 128 - wide)))
    more = gate_ref[...] + sums_in_lanes(spread_all, sums, 124)
    owned_ref[:, start : start + 128] = (low + more).astype(BF16)


def first_norm_back_body(near_ref, sib_ref, far_ref, x_ref, vector_ref, resid_grad_ref, out_ref):
    grad_n = near_ref[...].astype(F32) + sib_ref[...].astype(F32) + far_ref[...].astype(F32)
    normed, scaling = norm_stats(x_ref[...].astype(F32))
    out = resid_grad_ref[...] + norm_back(grad_n * vector_ref[0:1, :], normed, scaling)
    out_ref[...] = out.astype(BF16)


def second_sums_body(held, part, n_dp, got_ref, *refs):
    grad_refs, out_ref, gate_ref, sums_ref = refs[:3], *refs[3:]
    wide = got_ref.shape[1]
    got = got_ref[...].astype(F32).reshape(-1, 4, PAD, wide)
    total = jnp.sum(got, 0)
    last = -(-3 * part // 128) * 128
    for k in range(4):
        at = slice(k * part, (k + 1) * part)
        for m, ref in enumerate(grad_refs):
            ref[:, at] = total[k, :held, m * part : (m + 1) * part]
        out_ref[:, at] = total[k, :held, last : last + part]
    lanes = total[0] + total[1] + total[2] + total[3]
    lanes = lanes[:, last - 128 : last]
    first = 128 - 2 * n_dp
    gate_ref[...] = lanes[:held, first : first + n_dp]
    lane = iota(lanes.shape, 1)
    diagonal = iota(lanes.shape, 0) == lane
    for k, at in enumerate((124, 126, first + n_dp, first + n_dp + 2)):
        both = jnp.where((lane == at) | (lane == at + 1), lanes, 0.0)
        col_sum = jnp.sum(both, 1, keepdims=True)
        line = jnp.sum(jnp.where(diagonal, col_sum, 0.0), 0, keepdims=True)
        sums_ref[k : k + 1, :] = line[:, :held]


def layer_out_body(rows_ref, cols_ref, comb_ref, resid_ref, out_ref):
    slot = iota((cols_ref.shape[0], rows_ref.shape[0]), 1)
    out = resid_ref[...]
    for k in range(2):
        place = (slot == cols_ref[:, k : k + 1]).astype(F32).astype(BF16)
        out = out + comb_ref[:, k : k + 1] * mul(place, rows_ref[:, -out.shape[1] :])
    out_ref[...] = out.astype(BF16)


def per_device(
    tokens,
    bounds,
    routes,
    ln1_gain,
    ln1_bias,
    query_weight,
    key_weight,
    value_weight,
    output_weight,
    ln2_gain,
    ln2_bias,
    gate_new,
    gate_frozen,
    new_in,
    new_out,
    frozen_in,
    frozen_out,
    cotangent,
):
    rows, width = tokens.shape
    n_dp = lax.axis_size("dp")
    n_shard = lax.axis_size("shard")
    n_all = n_dp * n_shard
    held = query_weight.shape[0]
    padded = n_all * PAD
    group_len = rows * n_shard
    capacity = 2 * rows // n_dp
    slots = 2 * n_dp * capacity
    part = width // n_shard
    shard = lax.axis_index("shard")
    place = shard.reshape(1, 1)
    new_here = shard < n_shard // 2
    core_groups = [[2 * d + c for d in range(2 * n_dp)] for c in range(2)]
    pairs = [[0, 2], [1, 3]]
    spec_smem = pl.BlockSpec(memory_space=SMEM)
    spec_vmem = pl.BlockSpec(memory_space=VMEM)

    def swap(array, axis_groups=None):
        return lax.all_to_all(
            array, BOTH, split_axis=0, concat_axis=0, tiled=True, axis_index_groups=axis_groups
        )

    def dispatch(buffer):
        return swap(buffer.reshape(2 * n_dp, capacity, -1), core_groups).reshape(slots, -1)

    def send(array, step):
        return lax.ppermute(array, "shard", [(k, k ^ step) for k in range(n_shard)])

    def exchange(pieces):
        return [pieces[0]] + [send(piece, k) for k, piece in enumerate(pieces) if k > 0]

    x_far, x_sib = send(tokens, 2), send(tokens, 1)
    x_sib, query_weight = tie((x_sib, query_weight))

    half = width // 2
    wide = width + 128
    in_wide = -(-3 * part // 128) * 128
    last_wide = in_wide + 256
    (blocks,) = call(
        functools.partial(pack_body, part, in_wide),
        (shaped((n_dp, n_shard, PAD, in_wide + half), BF16),),
        (
            *(query_weight, key_weight, value_weight, output_weight, gate_new, gate_frozen),
            *(v[None] for v in (ln1_gain, ln1_bias, ln2_gain, ln2_bias)),
        ),
        scratch_shapes=[pltpu.VMEM((n_shard, PAD, in_wide + half), F32)],
    )
    blocks, x_far = tie((blocks, x_far))
    weights = swap(blocks.reshape(n_all, PAD, in_wide + half))
    x_last = send(x_far, 1)
    x_last, new_in, new_out, frozen_in, frozen_out = tie(
        (x_last, new_in, new_out, frozen_in, frozen_out)
    )
    x_parts = (tokens, x_sib, x_far, x_last)

    fresh, old = (new_in[0], new_out[0]), (frozen_in[0], frozen_out[0])
    own = [jnp.where(new_here, f, o) for f, o in zip(fresh, old)]
    away = jnp.stack([jnp.where(new_here, o, f) for f, o in zip(fresh, old)])
    sib_own = [send(array, 1) for array in own]

    cols, lines = call(
        functools.partial(slots_body, n_dp, capacity),
        (shaped((rows, 128), I32), shaped((8, rows), I32)),
        (routes, routes.T),
    )
    weights, x_parts, sib_own, lines, away = tie((weights, x_parts, sib_own, lines, away))
    far = lax.all_gather(away, "shard")
    in_got = weights[:, :, :in_wide].reshape(padded, in_wide)
    out_mine = weights[:, :, in_wide:].reshape(padded, half)

    w_in, vectors, n_one, qkv, *att, att_wide, log_total = call(
        functools.partial(attention_body, held),
        (
            shaped((width, in_wide), BF16),
            shaped((8, width), F32),
            shaped((group_len, width), BF16),
            shaped((group_len, in_wide), BF16),
            *[shaped((rows, part), BF16)] * 2,
            shaped((2 * rows, part), BF16),
            shaped((group_len, part), F32),
            shaped((8, group_len), F32),
        ),
        (bounds, place, in_got, *x_parts),
        in_specs=[spec_smem] * 2 + [spec_vmem] * 5,
    )
    out_sib = send(out_mine, 1)
    att_near, att_sib, att_far = att
    att_sib = send(att_sib, 1)
    att_sib, att_far = tie((att_sib, att_far))
    att_far = send(att_far, 2)
    att = att_near, att_sib, att_far, send(att_far, 1)

    w_out, resid, x_two, comb, buffer = call(
        functools.partial(router_body, held, n_dp),
        (
            shaped((width, width), BF16),
            shaped((rows, width), F32),
            shaped((rows, width), BF16),
            shaped((rows, 128), F32),
            shaped((slots, wide + width), BF16),
        ),
        (
            *(place, tokens, cotangent, *att, out_mine, out_sib),
            *(w_in, vectors, routes, lines),
        ),
        in_specs=[spec_smem] + [spec_vmem] * 12,
    )
    got = dispatch(buffer)

    back, grad_y, hidden, grad_pre = expert_call(place, got, (*own, *sib_own, far))
    back_got = dispatch(back)

    rows_t, grad_y_t = call(turn_body, (shaped((width, slots), BF16),) * 2, (got, grad_y))
    sent = weight_grads(rows_t, grad_y_t, hidden, grad_pre, 3, BF16)
    rows_t, sent = tie((rows_t, sent))
    sibs = [send(array, 1) for array in sent]
    sent_own = weight_grads(rows_t, grad_y_t, hidden, grad_pre, 2, BF16)
    rows_t, sent_own = tie((rows_t, sent_own))
    sibs_own = [send(array, 1) for array in sent_own]
    away_in, away_out = weight_grads(rows_t, grad_y_t, hidden, grad_pre, 1, BF16, sibs)
    far_in, far_out = (
        lax.all_gather(array, "shard", axis_index_groups=pairs) for array in (away_in, away_out)
    )
    own_new = weight_grads(rows_t, grad_y_t, hidden, grad_pre, 0, F32, sibs_own)
    back_got, own_new = tie((back_got, own_new))

    resid_grad, att_grad, gate_part = call(
        functools.partial(token_back_body, held, n_dp),
        (shaped((rows, width), F32), shaped((rows, width), BF16), shaped((padded, 128), F32)),
        (back_got, cols, routes, comb, cotangent, resid, x_two, w_in, vectors),
    )
    grad_far = send(att_grad, 2)
    grad_sib = send(att_grad, 1)
    layer_out = call(
        layer_out_body,
        shaped((rows, width), BF16),
        (back_got, cols, comb, resid),
    )
    grad_far, layer_out = tie((grad_far, layer_out))
    grad_last = send(grad_far, 1)
    extent = padded // n_shard
    head_grad, *out_pieces = call(
        functools.partial(projection_back_body, held),
        (shaped((group_len, part), BF16), *[shaped((extent, part), BF16)] * n_shard),
        (place, att_wide, w_out, att_grad, grad_sib, grad_far, grad_last),
        in_specs=[spec_smem] + [spec_vmem] * 6,
        scratch_shapes=[
            pltpu.VMEM((group_len, width), BF16),
            pltpu.VMEM((padded, part), BF16),
        ],
    )
    out_pieces = exchange(out_pieces)
    second_owned, *norm_part = call(
        functools.partial(attention_back_body, held),
        (shaped((padded, last_wide), BF16), *[shaped((rows, width), BF16)] * n_shard),
        (bounds, place, n_one, qkv, att_wide, log_total, w_in, gate_part, head_grad, *x_parts),
        in_specs=[spec_smem] * 2 + [spec_vmem] * 11,
        scratch_shapes=[
            pltpu.VMEM((group_len, 3 * part), BF16),
            pltpu.VMEM((group_len, part), F32),
            pltpu.VMEM((group_len, part), F32),
        ],
    )
    near_sib = send(norm_part[1], 1)
    far_sib = send(norm_part[3], 1)
    norm_far = send((norm_part[2].astype(F32) + far_sib.astype(F32)).astype(BF16), 2)
    second_owned = call(
        assemble_body,
        shaped((padded, last_wide), BF16),
        (place, second_owned, *out_pieces),
        grid=(2,),
        in_specs=[spec_smem, pl.BlockSpec(memory_space=pl.ANY)]
        + [pl.BlockSpec((extent, part), lambda c: (0, 0))] * n_shard,
        out_specs=pl.BlockSpec((padded, 128), lambda c: (0, in_wide // 128 + c)),
        input_output_aliases={1: 0},
    )
    second_got = swap(second_owned.reshape(n_all, PAD, last_wide)).reshape(padded, last_wide)
    grads_new = new_grads_call(place, own_new, far_in, far_out)
    norm_far, grads_new = tie((norm_far, grads_new))
    grad_tokens = call(
        first_norm_back_body,
        shaped((rows, width), BF16),
        (norm_part[0], near_sib, norm_far, tokens, vectors, resid_grad),
    )
    *grads_in, grad_out, grad_gate, ln_sums = call(
        functools.partial(second_sums_body, held, part, n_dp),
        (*[shaped((held, width), F32)] * 4, shaped((held, n_dp), F32), shaped((4, held), F32)),
        (second_got,),
    )
    return (
        *(layer_out, grad_tokens, *grads_in, grad_out),
        *(ln_sums[0], ln_sums[1], ln_sums[2], ln_sums[3]),
        *(grad_gate, *grads_new),
    )


def solution(mesh):
    flat = P(BOTH)
    lines = P(BOTH, None)
    in_specs = (
        (lines, P("dp", None), lines)
        + (flat, flat)
        + (lines,) * 4
        + (flat, flat, lines, lines)
        + (P("dp", None, "shard"), P("dp", "shard", None)) * 2
        + (lines,)
    )
    out_specs = (
        (lines,) * 6
        + (flat,) * 4
        + (lines, P("dp", None, "shard"), P("dp", "shard", None))
    )
    return jax.shard_map(
        per_device, mesh=mesh, in_specs=in_specs, out_specs=out_specs, check_vma=False
    )
```

```python
import functools

import jax
import jax.numpy as jnp
from jax import lax
from jax.experimental import pallas as pl
from jax.experimental.pallas import tpu as pltpu
from jax.sharding import PartitionSpec as P

HEAD_DIM = 64
BOTH = ("dp", "shard")
F32 = jnp.float32
BF16 = jnp.bfloat16
I32 = jnp.int32
VMEM_BYTES = 56 * 2**20
PAD = 8
SMEM = pltpu.SMEM
VMEM = pltpu.VMEM


def mul(left, right):
    return jnp.dot(left, right, preferred_element_type=F32)


def contract_rows(left, right):
    return lax.dot_general(left, right, (((0,), (0,)), ((), ())), preferred_element_type=F32)


def contract_cols(left, right):
    return lax.dot_general(left, right, (((1,), (1,)), ((), ())), preferred_element_type=F32)


def iota(shape, dim):
    return lax.broadcasted_iota(I32, shape, dim)


def norm_stats(values_in):
    center = values_in - jnp.mean(values_in, -1, keepdims=True)
    scaling = lax.rsqrt(jnp.mean(center * center, -1, keepdims=True) + 1e-05)
    return (center * scaling, scaling)


def norm_back(grad_normed, normed, scaling):
    mean_grad = jnp.mean(grad_normed, -1, keepdims=True)
    mean_cross = jnp.mean(grad_normed * normed, -1, keepdims=True)
    return scaling * (grad_normed - mean_grad - normed * mean_cross)


def in_three(values_in):
    first = values_in.astype(BF16).astype(F32)
    rest = values_in - first
    second = rest.astype(BF16).astype(F32)
    return first, second, rest - second


def in_lanes(terms, rows):
    lane = iota((rows, 128), 1)
    out = jnp.zeros((rows, 128), F32)
    for k, term in enumerate(terms):
        out = jnp.where(lane == k, term, out)
    return out


def spread(held, width, rows_first):
    padded = width // held * PAD
    shape, row_dim = ((width, padded), 0) if rows_first else ((padded, width), 1)
    row, col = iota(shape, row_dim), iota(shape, 1 - row_dim)
    block = block_of(row, held)
    return (col == block * PAD + (row - block * held)).astype(F32).astype(BF16)


def block_of(row, held):
    step = -(-(1 << 16) // held)
    return lax.shift_right_logical(row * step, 16)


def vector_rows(lanes, held, width, which, first=0):
    row = iota((lanes.shape[1], width), 1)
    lane = iota((lanes.shape[1], width), 0) - first
    pick = (lane == row - block_of(row, held) * held).astype(F32)
    wide = mul(lanes, pick.astype(BF16))
    col = iota(wide.shape, 1)
    wanted = iota(wide.shape, 0) == block_of(col, held) * PAD + which
    return jnp.sum(jnp.where(wanted, wide, 0.0), 0, keepdims=True)


def call(body, out_shapes, args, **more):
    return pl.pallas_call(
        body,
        out_shape=out_shapes,
        compiler_params=pltpu.CompilerParams(vmem_limit_bytes=VMEM_BYTES),
        cost_estimate=pl.CostEstimate(flops=1, bytes_accessed=1, transcendentals=1),
        **more,
    )(*args)


tie = lax.optimization_barrier


def shaped(shape, dtype):
    return jax.ShapeDtypeStruct(shape, dtype)


def pack_body(part, in_wide, query_ref, key_ref, value_ref, out_ref, new_ref, old_ref, *refs):
    (gain_one, bias_one, gain_two, bias_two), blocks_ref, work_ref = refs[:4], refs[4], refs[5]
    held, width = out_ref.shape
    half, gates, at = width // 2, new_ref.shape[1], 3 * part
    work_ref[...] = jnp.zeros_like(work_ref)
    for k in range(work_ref.shape[0]):
        for m, ref in enumerate((query_ref, key_ref, value_ref)):
            piece = ref[:, k * part : (k + 1) * part]
            work_ref[k, :held, m * part : (m + 1) * part] = piece.astype(F32)
        work_ref[k, :held, at : at + gates] = new_ref[...].astype(F32)
        work_ref[k, :held, at + gates : at + 2 * gates] = old_ref[...].astype(F32)
        side = out_ref[:, k % 2 * half : (k % 2 + 1) * half]
        work_ref[k, :held, in_wide : in_wide + half] = side.astype(F32)
        work_ref[k, held : held + 1, :held] = gain_one[...].astype(F32)
        work_ref[k, held + 1 : held + 2, :held] = bias_one[...].astype(F32)
        work_ref[k, held : held + 1, at : at + held] = gain_two[...].astype(F32)
        work_ref[k, held + 1 : held + 2, at : at + held] = bias_two[...].astype(F32)
    blocks = work_ref[...].astype(BF16)

    def put(k, carry):
        blocks_ref[k] = blocks
        return carry

    lax.fori_loop(0, blocks_ref.shape[0], put, 0)


def slots_body(n_dp, capacity, routes_ref, routes_t_ref, cols_ref, lines_ref):
    rows = routes_ref.shape[0]
    routes = routes_ref[...]
    hot = [
        (iota((rows, 2 * n_dp), 1) == routes[:, k : k + 1]).astype(F32) for k in range(2)
    ]
    earlier = (iota((rows, rows), 1) < iota((rows, rows), 0)).astype(F32).astype(BF16)
    count = mul(earlier, (hot[0] + hot[1]).astype(BF16))
    expert = routes
    base = jnp.where(expert < n_dp, 2 * expert, 2 * expert - 2 * n_dp + 1) * capacity
    cols = [
        base[:, k : k + 1] + jnp.sum(count * hot[k], 1, keepdims=True).astype(I32)
        for k in range(2)
    ]
    lane = iota(cols_ref.shape, 1)
    cols_ref[...] = jnp.where(lane == 0, cols[0], cols[1])
    routes_t = routes_t_ref[...]
    hot_t = [
        (iota((2 * n_dp, rows), 0) == routes_t[k : k + 1]).astype(F32) for k in range(2)
    ]
    later = (iota((rows, rows), 0) < iota((rows, rows), 1)).astype(F32).astype(BF16)
    count_t = mul((hot_t[0] + hot_t[1]).astype(BF16), later)
    base_t = jnp.where(routes_t < n_dp, 2 * routes_t, 2 * routes_t - 2 * n_dp + 1) * capacity
    lines = [
        base_t[k : k + 1] + jnp.sum(count_t * hot_t[k], 0, keepdims=True).astype(I32)
        for k in range(2)
    ]
    sub = iota(lines_ref.shape, 0)
    lines_ref[...] = jnp.where(sub == 0, lines[0], lines[1])


def seen_bias(bounds_ref, first, rows, keys, turned=False):
    query = iota((1, rows) if turned else (rows, 1), int(turned)) + first
    key = iota((keys, 1) if turned else (1, keys), 1 - int(turned))
    start, end = bounds_ref[0, 0], bounds_ref[0, 1]

    def doc(pos):
        return (pos >= start).astype(I32) + (pos >= end).astype(I32)

    seen = (doc(query) == doc(key)) & (key <= query)
    return jnp.where(seen, 0.0, -1e30)


def prepare_body(held, shard_ref, *refs):
    x_refs, normed_ref, spread_ref = refs[:4], refs[4], refs[5]
    tile, width = x_refs[0].shape
    for k, x_ref in enumerate(x_refs):
        at = pl.ds(pl.multiple_of((shard_ref[0, 0] ^ k) * tile, tile), tile)
        normed_ref[at, :], unused = norm_stats(x_ref[...].astype(F32))
    spread_ref[...] = spread(held, width, True)


def attention_body(held, bounds_ref, shard_ref, got_ref, normed_ref, spread_ref, *refs):
    (weight_ref, vector_ref, n_ref, qkv_ref), refs = refs[:4], refs[4:]
    near_ref, sib_ref, far_ref, att_wide_ref, total_ref = refs
    width = normed_ref.shape[1]
    tile = normed_ref.shape[0] // 4
    part = att_wide_ref.shape[1]
    shard = shard_ref[0, 0]
    got = got_ref[...]
    weight_ref[...] = mul(spread_ref[...], got).astype(BF16)
    lanes, last = got[:, :128], got[:, got.shape[1] - 128 :]
    first = 3 * part - (got.shape[1] - 128)
    gain = vector_rows(lanes, held, width, held)
    bias = vector_rows(lanes, held, width, held + 1)
    sub = iota(vector_ref.shape, 0)
    vectors = jnp.where(sub == 0, gain, bias)
    vectors = jnp.where(sub == 2, vector_rows(last, held, width, held, first), vectors)
    vector_ref[...] = jnp.where(
        sub == 3, vector_rows(last, held, width, held + 1, first), vectors
    )
    for block in range(4):
        at = slice(block * tile, (block + 1) * tile)
        n_one = (normed_ref[at, :] * gain + bias).astype(BF16)
        n_ref[at, :] = n_one
        out = mul(n_one, weight_ref[...])
        scale = jnp.where(iota(out.shape, 1) < part, HEAD_DIM ** (-0.5), 1.0)
        qkv_ref[at, :] = (out.astype(BF16).astype(F32) * scale).astype(BF16)
    for block in range(4):
        first, keys = block * tile, (block + 1) * tile
        hidden = seen_bias(bounds_ref, first, tile, keys)
        totals = []
        for head in range(part // HEAD_DIM):
            at = head * HEAD_DIM
            query = qkv_ref[first:keys, at : at + HEAD_DIM]
            key = qkv_ref[0:keys, part + at : part + at + HEAD_DIM]
            value = qkv_ref[0:keys, 2 * part + at : 2 * part + at + HEAD_DIM]
            scores = contract_cols(query, key) + hidden
            highest = jnp.max(scores, 1, keepdims=True)
            exponent = jnp.exp(scores - highest)
            total = jnp.sum(exponent, 1, keepdims=True)
            prob = (exponent * (1.0 / total)).astype(BF16)
            att_wide_ref[first:keys, at : at + HEAD_DIM] = mul(prob, value)
            totals.append(highest + jnp.log(total))
        total_ref[:, first:keys] = in_lanes(totals, tile).T[: total_ref.shape[0]]
    for k, put in enumerate((near_ref, sib_ref, far_ref.at[:tile], far_ref.at[tile:])):
        at = pl.ds(pl.multiple_of((shard ^ k) * tile, tile), tile)
        put[...] = att_wide_ref[at, :].astype(BF16)


def unpack_body(shard_ref, mine_ref, other_ref, spread_ref, lines_ref, weight_ref, place_ref):
    first_core = shard_ref[0, 0] % 2 == 0
    half = mine_ref.shape[1]
    left = jnp.where(first_core, mine_ref[...], other_ref[...])
    right = jnp.where(first_core, other_ref[...], mine_ref[...])
    weight_ref[:, :half] = mul(spread_ref[...], left).astype(BF16)
    weight_ref[:, half:] = mul(spread_ref[...], right).astype(BF16)
    slot = iota(place_ref.shape[1:], 0)
    for k in range(2):
        place_ref[k] = (slot == lines_ref[k : k + 1, :]).astype(F32).astype(BF16)


def router_body(
    n_dp,
    shard_ref,
    x_ref,
    grad_ref,
    near_ref,
    sib_ref,
    far_ref,
    last_ref,
    weight_ref,
    gates_ref,
    vector_ref,
    routes_ref,
    place_ref,
    resid_ref,
    x_two_ref,
    comb_ref,
    out_ref,
):
    rows, width = x_ref.shape
    part = near_ref.shape[1]
    shard = shard_ref[0, 0]
    gain, bias = vector_ref[2:3, :], vector_ref[3:4, :]
    resid = x_ref[...].astype(F32)
    for k, ref in enumerate((near_ref, sib_ref, far_ref.at[:rows], last_ref.at[rows:])):
        at = pl.ds(pl.multiple_of((shard ^ k) * part, part), part)
        resid = resid + mul(ref[...], weight_ref[at, :])
    resid_ref[...] = resid
    normed, unused = norm_stats(resid)
    x_two = (normed * gain + bias).astype(BF16)
    x_two_ref[...] = x_two
    logits = mul(x_two, gates_ref[:, gates_ref.shape[1] - 128 :])
    lane = iota(logits.shape, 1) - (128 - 2 * n_dp)
    chosen = [
        jnp.sum(jnp.where(lane == routes_ref[:, k : k + 1], logits, 0.0), 1, keepdims=True)
        for k in range(2)
    ]
    top = jnp.maximum(chosen[0], chosen[1])
    raw = [jnp.exp(c - top) for c in chosen]
    comb = [r / (raw[0] + raw[1]) for r in raw]
    comb_ref[...] = in_lanes(comb, rows)
    place = [place_ref[k] for k in range(2)]
    both = place[0] + place[1]
    out_ref[:, :width] = mul(both, x_two).astype(BF16)
    terms = [in_lanes(in_three(c), rows).astype(BF16) for c in comb]
    placed = mul(place[0], terms[0]) + mul(place[1], terms[1])
    out_ref[:, width : width + 128] = placed.astype(BF16)
    out_ref[:, width + 128 :] = mul(both, grad_ref[...]).astype(BF16)


def expert_body(
    shard_ref,
    rows_ref,
    *refs,
):
    own_refs, sib_refs, far_refs = refs[:2], refs[2:4], refs[4:6]
    back_ref, grad_y_ref, hidden_ref, grad_pre_ref = refs[6:10]
    held_ref, hid_ref, pre_ref, sum_out_ref, sum_back_ref, sems, out_sems = refs[10:]
    slots, width = grad_y_ref.shape
    wide = width + 128
    chunk = 256
    pieces = [slice(k * chunk, (k + 1) * chunk) for k in range(width // chunk)]
    shard = shard_ref[0, 0]
    sources = (
        own_refs,
        [ref.at[shard ^ 2] for ref in far_refs],
        sib_refs,
        [ref.at[shard ^ 3] for ref in far_refs],
    )
    copies = [
        [
            pltpu.make_async_copy(ref, held_ref.at[k, m], sems.at[k, m])
            for m, ref in enumerate(parts)
        ]
        for k, parts in enumerate(sources)
    ]
    for copy in sum(copies, []):
        copy.start()
    comb = jnp.sum(rows_ref[:, width:wide].astype(F32), 1, keepdims=True)
    grad_y_ref[...] = (comb * rows_ref[:, wide:].astype(F32)).astype(BF16)

    def hide(q, at):
        pre = mul(rows_ref[:, :width], held_ref[q, 0, :, at])
        grad_hidden = contract_cols(grad_y_ref[...], held_ref[q, 1, at, :])
        square = pre * pre
        tanh = jnp.tanh(pre * (0.7978845608028654 + 0.035677408136300125 * square))
        share = 0.5 + 0.5 * tanh
        hid = pre * share
        hid_ref[q, :, at] = hid.astype(BF16)
        slope = share + (hid * (1.0 - share)) * (
            1.5957691216057308 + 0.21406444881780074 * square
        )
        pre_ref[q, :, at] = (grad_hidden * slope).astype(BF16)

    def join(q, at):
        out = mul(hid_ref[q], held_ref[q, 1, :, at])
        back = contract_cols(pre_ref[q], held_ref[q, 0, at, :])
        return out, back

    def saves(q):
        at = pl.ds(pl.multiple_of(q * width, width), width)
        return (
            pltpu.make_async_copy(hid_ref.at[q], hidden_ref.at[:, at], out_sems.at[0, q]),
            pltpu.make_async_copy(pre_ref.at[q], grad_pre_ref.at[:, at], out_sems.at[1, q]),
        )

    for copy in copies[0]:
        copy.wait()
    for at in pieces:
        hide(0, at)
    for k, group in enumerate(copies[1:]):
        for copy in group:
            copy.wait()
        for save in saves(k):
            save.start()
        for at in pieces:
            hide(k + 1, at)
            out, back = join(k, at)
            if k == 0:
                sum_out_ref[:, at] = out
                sum_back_ref[:, at] = back
            else:
                sum_out_ref[:, at] += out
                sum_back_ref[:, at] += back
    last = len(copies) - 1
    for save in saves(last):
        save.start()
    dcomb = jnp.zeros((slots, 1), F32)
    for at in pieces:
        out, back = join(last, at)
        out = (sum_out_ref[:, at] + out).astype(BF16)
        back_ref[:, at] = (sum_back_ref[:, at] + back).astype(BF16)
        last_at = slice(wide + at.start, wide + at.stop)
        back_ref[:, last_at] = out
        dcomb += jnp.sum(rows_ref[:, last_at].astype(F32) * out.astype(F32), 1, keepdims=True)
    back_ref[:, width:wide] = in_lanes(in_three(dcomb), slots).astype(BF16)
    for k in range(len(copies)):
        for save in saves(k):
            save.wait()


def expert_call(shard, rows, weights):
    slots = rows.shape[0]
    width = quarter = weights[0].shape[1]
    inside = pl.BlockSpec(memory_space=VMEM)
    anywhere = pl.BlockSpec(memory_space=pl.ANY)
    return call(
        expert_body,
        (
            shaped(rows.shape, BF16),
            shaped((slots, width), BF16),
            shaped((slots, 4 * quarter), BF16),
            shaped((slots, 4 * quarter), BF16),
        ),
        (shard, rows, *weights),
        in_specs=[pl.BlockSpec(memory_space=SMEM), inside] + [anywhere] * len(weights),
        out_specs=[inside] * 2 + [anywhere] * 2,
        scratch_shapes=[
            pltpu.VMEM((4, 2, quarter, quarter), BF16),
            pltpu.VMEM((4, slots, quarter), BF16),
            pltpu.VMEM((4, slots, quarter), BF16),
            pltpu.VMEM((slots, width), F32),
            pltpu.VMEM((slots, width), F32),
            pltpu.SemaphoreType.DMA((4, 2)),
            pltpu.SemaphoreType.DMA((2, 4)),
        ],
    )


def turn_body(rows_ref, grad_y_ref, rows_t_ref, grad_y_t_ref):
    rows_t_ref[...] = rows_ref[:, : rows_t_ref.shape[0]].T
    grad_y_t_ref[...] = grad_y_ref[...].T


def weight_grad_body(rows_t_ref, grad_y_t_ref, hidden_ref, grad_pre_ref, *refs):
    grads = [
        mul(rows_t_ref[...], grad_pre_ref[...]),
        mul(grad_y_t_ref[...], hidden_ref[...]),
    ]
    if len(refs) > 2:
        grads = [grad + ref[...].astype(F32) for grad, ref in zip(grads, refs)]
    if len(refs) == 3:
        refs[2][0], refs[2][1] = (grad.astype(BF16) for grad in grads)
        return
    for grad, ref in zip(grads, refs[-2:]):
        ref[...] = grad.astype(ref.dtype)


def weight_grads(rows_t, grad_y_t, hidden, grad_pre, which, dtype, sibs=(), stacked=False):
    width, slots = grad_y_t.shape
    quarter = hidden.shape[1] // 4
    chunk = 256
    pieces = quarter // chunk
    whole = pl.BlockSpec((width, slots), lambda c: (0, 0))
    piece = pl.BlockSpec((slots, chunk), lambda c: (0, which * pieces + c))
    shapes = (shaped((width, quarter), dtype),) * 2
    out_specs = [pl.BlockSpec((width, chunk), lambda c: (0, c))] * 2
    if stacked:
        shapes = shaped((2, width, quarter), dtype)
        out_specs = pl.BlockSpec((2, width, chunk), lambda c: (0, 0, c))
    return call(
        weight_grad_body,
        shapes,
        (rows_t, grad_y_t, hidden, grad_pre, *sibs),
        grid=(pieces,),
        in_specs=[whole] * 2
        + [piece] * 2
        + [pl.BlockSpec((width, chunk), lambda c: (0, c))] * len(sibs),
        out_specs=out_specs,
    )


def new_grads_body(shard_ref, in_ref, out_ref, far_ref, grad_in_ref, grad_out_ref):
    new_here = shard_ref[0, 0] < 2
    grad_in_ref[0] = jnp.where(new_here, in_ref[...], far_ref[0, 0].astype(F32))
    grad_out_ref[0] = jnp.where(new_here, out_ref[...], far_ref[0, 1].astype(F32)).T


def new_grads_call(shard, own, far):
    quarter = own[0].shape[0]
    tile = quarter // 3
    piece = pl.BlockSpec((quarter, tile), lambda c: (0, c))
    one = pl.BlockSpec((1, quarter, tile), lambda c: (0, 0, c))
    return call(
        new_grads_body,
        (shaped((1, quarter, quarter), F32),) * 2,
        (shard, *own, far),
        grid=(3,),
        in_specs=[pl.BlockSpec(memory_space=SMEM), piece, piece]
        + [pl.BlockSpec((1, 2, quarter, tile), lambda c: (0, 0, 0, c))],
        out_specs=[one, pl.BlockSpec((1, tile, quarter), lambda c: (0, c, 0))],
    )


def token_back_body(
    n_dp,
    back_ref,
    cols_ref,
    routes_ref,
    comb_ref,
    grad_ref,
    resid_ref,
    gates_ref,
    vector_ref,
    resid_grad_ref,
    att_ref,
    dlogits_ref,
    sums_ref,
):
    rows, width = grad_ref.shape
    slots = back_ref.shape[0]
    slot = iota((rows, slots), 1)
    back = [
        mul(
            (slot == cols_ref[:, k : k + 1]).astype(F32).astype(BF16),
            back_ref[:, : width + 128],
        )
        for k in range(2)
    ]
    dcomb = [jnp.sum(b[:, width:], 1, keepdims=True) for b in back]
    comb = [comb_ref[:, k : k + 1] for k in range(2)]
    mean = comb[0] * dcomb[0] + comb[1] * dcomb[1]
    dlog = [c * (d - mean) for c, d in zip(comb, dcomb)]
    lane = iota((rows, 128), 1) - (128 - 2 * n_dp)
    dlogits = jnp.where(lane == routes_ref[:, 0:1], dlog[0], 0.0)
    dlogits = jnp.where(lane == routes_ref[:, 1:2], dlog[1], dlogits).astype(BF16)
    gate = gates_ref[:, gates_ref.shape[1] - 128 :]
    grad_x_two = contract_cols(dlogits, gate) + back[0][:, :width] + back[1][:, :width]
    normed, scaling = norm_stats(resid_ref[...])
    sums = [jnp.sum(grad_x_two * normed, 0, keepdims=True), jnp.sum(grad_x_two, 0, keepdims=True)]
    gain = vector_ref[2:3, :]
    grad_resid = grad_ref[...].astype(F32) + norm_back(grad_x_two * gain, normed, scaling)
    resid_grad_ref[...] = grad_resid
    att_ref[...] = grad_resid.astype(BF16)
    dlogits_ref[...] = dlogits
    sub = iota(sums_ref.shape, 0)
    sums_ref[...] = jnp.where(sub == 0, sums[0], sums[1])


def sums_in_lanes(spread_all, sums, first):
    sub = iota((128, sums[0].shape[1]), 0)
    lines = jnp.zeros(sub.shape, F32)
    for k, row in enumerate(sums):
        high, low, unused = in_three(row)
        lines = jnp.where(sub == first + 2 * k, high, lines)
        lines = jnp.where(sub == first + 2 * k + 1, low, lines)
    return contract_cols(spread_all, lines.astype(BF16))


def projection_back_body(
    held,
    shard_ref,
    att_ref,
    weight_ref,
    near_ref,
    sib_ref,
    far_ref,
    far_sib_ref,
    grad_ref,
    *refs,
):
    out_refs, all_ref, owned_ref = refs[:4], *refs[4:]
    tile, width = near_ref.shape
    part = att_ref.shape[1]
    shard = shard_ref[0, 0]
    for k, ref in enumerate((near_ref, sib_ref, far_ref, far_sib_ref)):
        at = pl.ds(pl.multiple_of((shard ^ k) * tile, tile), tile)
        all_ref[at, :] = ref[...]
    mine = pl.ds(pl.multiple_of(shard * part, part), part)
    grad_ref[...] = contract_cols(all_ref[...], weight_ref[mine, :]).astype(BF16)
    turned = contract_cols(spread(held, part, False), att_ref[...].astype(BF16)).astype(BF16)
    owned = mul(turned, all_ref[...]).astype(BF16)
    extent = owned.shape[0]
    for k in range(width // part):
        owned_ref[k * extent : (k + 1) * extent, :] = owned[:, k * part : (k + 1) * part]
    for k, out_ref in enumerate(out_refs):
        at = pl.ds(pl.multiple_of((shard ^ k) * extent, extent), extent)
        out_ref[...] = owned_ref[at, :]


def assemble_body(shard_ref, all_ref, near_ref, sib_ref, far_ref, last_ref, out_ref):
    rows, part = near_ref.shape
    shard = shard_ref[0, 0]
    step = pl.program_id(0)
    for k, ref in enumerate((near_ref, sib_ref, far_ref, last_ref)):
        at = pl.ds(pl.multiple_of((shard ^ k) * rows, rows), rows)

        @pl.when(step == 0)
        def _(at=at, ref=ref):
            out_ref[at, :] = ref[:, :128]

        @pl.when(step == 1)
        def _(at=at, ref=ref):
            out_ref[at, : part - 128] = ref[:, 128:]
            out_ref[at, part - 128 :] = jnp.zeros((rows, 256 - part), BF16)


def attention_back_body(
    held,
    bounds_ref,
    shard_ref,
    n_ref,
    qkv_ref,
    att_ref,
    total_ref,
    weight_ref,
    gate_ref,
    grad_ref,
    *refs,
):
    normed_ref, owned_ref, part_refs = refs[0], refs[1], refs[2:6]
    grads_ref, key_ref, value_ref = refs[6:]
    tile, width = normed_ref.shape[0] // 4, normed_ref.shape[1]
    part = att_ref.shape[1]
    shard = shard_ref[0, 0]
    key_ref[...] = jnp.zeros_like(key_ref)
    value_ref[...] = jnp.zeros_like(value_ref)
    heads = part // HEAD_DIM
    for block in range(4):
        first, keys = block * tile, (block + 1) * tile
        hidden = seen_bias(bounds_ref, first, tile, keys, True)
        product = grad_ref[first:keys, :].astype(F32) * att_ref[first:keys, :]
        deltas = [
            jnp.sum(product[:, k * HEAD_DIM : (k + 1) * HEAD_DIM], 1, keepdims=True)
            for k in range(heads)
        ]
        deltas = in_lanes(deltas, tile).T
        queries = []
        for head in range(heads):
            at = head * HEAD_DIM
            mine = slice(at, at + HEAD_DIM)
            query = qkv_ref[first:keys, mine]
            key = qkv_ref[0:keys, part + at : part + at + HEAD_DIM]
            value = qkv_ref[0:keys, 2 * part + at : 2 * part + at + HEAD_DIM]
            grad = grad_ref[first:keys, mine]
            scores = contract_cols(key, query) + hidden
            prob = jnp.exp(scores - total_ref[head : head + 1, first:keys])
            grad_prob = contract_cols(value, grad)
            grad_score = (prob * (grad_prob - deltas[head : head + 1])).astype(BF16)
            queries.append(contract_rows(key, grad_score) * HEAD_DIM ** (-0.5))
            key_ref[0:keys, mine] += mul(grad_score, query)
            value_ref[0:keys, mine] += mul(prob.astype(BF16), grad)
        grads_ref[first:keys, :part] = jnp.concatenate(queries, 0).T.astype(BF16)
    grads_ref[:, part : 2 * part] = key_ref[...].astype(BF16)
    grads_ref[:, 2 * part :] = value_ref[...].astype(BF16)
    sums = [jnp.zeros((1, width), F32)] * 2
    for k, part_ref in enumerate(part_refs):
        at = pl.ds(pl.multiple_of((shard ^ k) * tile, tile), tile)
        grad_n = contract_cols(grads_ref[at, :], weight_ref[:, : 3 * part])
        part_ref[...] = grad_n.astype(BF16)
        sums[0] += jnp.sum(grad_n * normed_ref[at, :], 0, keepdims=True)
        sums[1] += jnp.sum(grad_n, 0, keepdims=True)
    spread_all = spread(held, width, False)
    wide = 3 * part
    owned = jnp.zeros((spread_all.shape[0], wide), F32)
    for block in range(4):
        at = slice(block * tile, (block + 1) * tile)
        turned = contract_cols(spread_all, n_ref[at, :]).astype(BF16)
        owned += mul(turned, grads_ref[at, :])
    start = -(-wide // 128) * 128 - 128
    owned_ref[:, :start] = owned[:, :start].astype(BF16)
    low = jnp.pad(owned[:, start:], ((0, 0), (0, start + 128 - wide)))
    more = gate_ref[...] + sums_in_lanes(spread_all, sums, 124)
    owned_ref[:, start : start + 128] = (low + more).astype(BF16)


def first_norm_back_body(near_ref, sib_ref, far_ref, x_ref, vector_ref, resid_grad_ref, out_ref):
    grad_n = near_ref[...].astype(F32) + sib_ref[...].astype(F32) + far_ref[...].astype(F32)
    normed, scaling = norm_stats(x_ref[...].astype(F32))
    out = resid_grad_ref[...] + norm_back(grad_n * vector_ref[0:1, :], normed, scaling)
    out_ref[...] = out.astype(BF16)


def second_sums_body(held, part, n_dp, got_ref, *refs):
    grad_refs, out_ref, gate_ref, sums_ref = refs[:3], *refs[3:]
    wide = got_ref.shape[1]
    got = got_ref[...].astype(F32).reshape(-1, 4, PAD, wide)
    total = jnp.sum(got, 0)
    last = -(-3 * part // 128) * 128
    for k in range(4):
        at = slice(k * part, (k + 1) * part)
        for m, ref in enumerate(grad_refs):
            ref[:, at] = total[k, :held, m * part : (m + 1) * part]
        out_ref[:, at] = total[k, :held, last : last + part]
    lanes = total[0] + total[1] + total[2] + total[3]
    lanes = lanes[:, last - 128 : last]
    first = 128 - 2 * n_dp
    gate_ref[...] = lanes[:held, first : first + n_dp]
    lane = iota(lanes.shape, 1)
    diagonal = iota(lanes.shape, 0) == lane
    for k, at in enumerate((124, 126, first + n_dp, first + n_dp + 2)):
        both = jnp.where((lane == at) | (lane == at + 1), lanes, 0.0)
        col_sum = jnp.sum(both, 1, keepdims=True)
        line = jnp.sum(jnp.where(diagonal, col_sum, 0.0), 0, keepdims=True)
        sums_ref[k : k + 1, :] = line[:, :held]


def layer_out_body(
    held,
    n_dp,
    rows_ref,
    cols_ref,
    comb_ref,
    resid_ref,
    x_two_ref,
    dlogits_ref,
    sums_ref,
    out_ref,
    gate_ref,
):
    slot = iota((cols_ref.shape[0], rows_ref.shape[0]), 1)
    out = resid_ref[...]
    for k in range(2):
        place = (slot == cols_ref[:, k : k + 1]).astype(F32).astype(BF16)
        out = out + comb_ref[:, k : k + 1] * mul(place, rows_ref[:, -out.shape[1] :])
    out_ref[...] = out.astype(BF16)
    spread_all = spread(held, out.shape[1], False)
    turned = contract_cols(spread_all, x_two_ref[...]).astype(BF16)
    dlogits = dlogits_ref[...].astype(F32)
    lane = iota(dlogits.shape, 1) - (128 - 2 * n_dp)
    own_gates = jnp.where(lane < n_dp, dlogits, 0.0).astype(BF16)
    sums = [sums_ref[0:1, :], sums_ref[1:2, :]]
    gate_ref[...] = mul(turned, own_gates) + sums_in_lanes(spread_all, sums, 128 - n_dp)


def per_device(
    tokens,
    bounds,
    routes,
    ln1_gain,
    ln1_bias,
    query_weight,
    key_weight,
    value_weight,
    output_weight,
    ln2_gain,
    ln2_bias,
    gate_new,
    gate_frozen,
    new_in,
    new_out,
    frozen_in,
    frozen_out,
    cotangent,
):
    rows, width = tokens.shape
    n_dp = lax.axis_size("dp")
    n_shard = lax.axis_size("shard")
    n_all = n_dp * n_shard
    held = query_weight.shape[0]
    padded = n_all * PAD
    group_len = rows * n_shard
    capacity = 2 * rows // n_dp
    slots = 2 * n_dp * capacity
    part = width // n_shard
    shard = lax.axis_index("shard")
    place = shard.reshape(1, 1)
    new_here = shard < n_shard // 2
    core_groups = [[2 * d + c for d in range(2 * n_dp)] for c in range(2)]
    pairs = [[0, 2], [1, 3]]
    spec_smem = pl.BlockSpec(memory_space=SMEM)
    spec_vmem = pl.BlockSpec(memory_space=VMEM)

    def swap(array, axis_groups=None):
        return lax.all_to_all(
            array, BOTH, split_axis=0, concat_axis=0, tiled=True, axis_index_groups=axis_groups
        )

    def dispatch(buffer):
        return swap(buffer.reshape(2 * n_dp, capacity, -1), core_groups).reshape(slots, -1)

    def send(array, step):
        return lax.ppermute(array, "shard", [(k, k ^ step) for k in range(n_shard)])

    def exchange(pieces):
        return [pieces[0]] + [send(piece, k) for k, piece in enumerate(pieces) if k > 0]

    x_far, x_sib = send(tokens, 2), send(tokens, 1)
    x_sib, new_in, new_out, frozen_in, frozen_out, query_weight = tie(
        (x_sib, new_in, new_out, frozen_in, frozen_out, query_weight)
    )

    half = width // 2
    wide = width + 128
    in_wide = -(-3 * part // 128) * 128
    last_wide = in_wide + 256
    (blocks,) = call(
        functools.partial(pack_body, part, in_wide),
        (shaped((n_dp, n_shard, PAD, in_wide + half), BF16),),
        (
            *(query_weight, key_weight, value_weight, output_weight, gate_new, gate_frozen),
            *(v[None] for v in (ln1_gain, ln1_bias, ln2_gain, ln2_bias)),
        ),
        scratch_shapes=[pltpu.VMEM((n_shard, PAD, in_wide + half), F32)],
    )
    fresh, old = (new_in[0], new_out[0]), (frozen_in[0], frozen_out[0])
    own = [jnp.where(new_here, f, o) for f, o in zip(fresh, old)]
    away = [jnp.where(new_here, o, f) for f, o in zip(fresh, old)]
    blocks, x_far, own, away = tie((blocks, x_far, own, away))
    weights = swap(blocks.reshape(n_all, PAD, in_wide + half))
    far = [lax.all_gather(array, "shard") for array in away]
    sib_own = [send(array, 1) for array in own]
    x_parts = (tokens, x_sib, x_far, send(x_far, 1))

    cols, lines = call(
        functools.partial(slots_body, n_dp, capacity),
        (shaped((rows, 128), I32), shaped((8, rows), I32)),
        (routes, routes.T),
    )
    normed_one, spread_all = call(
        functools.partial(prepare_body, held),
        (shaped((group_len, width), F32), shaped((width, padded), BF16)),
        (place, *x_parts),
        in_specs=[spec_smem] + [spec_vmem] * 4,
    )
    weights, normed_one, sib_own, lines = tie((weights, normed_one, sib_own, lines))
    in_got = weights[:, :, :in_wide].reshape(padded, in_wide)
    out_mine = weights[:, :, in_wide:].reshape(padded, half)

    w_in, vectors, n_one, qkv, *att, att_wide, log_total = call(
        functools.partial(attention_body, held),
        (
            shaped((width, in_wide), BF16),
            shaped((8, width), F32),
            shaped((group_len, width), BF16),
            shaped((group_len, in_wide), BF16),
            *[shaped((rows, part), BF16)] * 2,
            shaped((2 * rows, part), BF16),
            shaped((group_len, part), F32),
            shaped((8, group_len), F32),
        ),
        (bounds, place, in_got, normed_one, spread_all),
        in_specs=[spec_smem] * 2 + [spec_vmem] * 3,
    )
    out_sib = send(out_mine, 1)
    att_near, att_sib, att_far = att
    att_sib = send(att_sib, 1)
    att_sib, att_far = tie((att_sib, att_far))
    att_far = send(att_far, 2)
    w_out, place_map = call(
        unpack_body,
        (shaped((width, width), BF16), shaped((2, slots, rows), BF16)),
        (place, out_mine, out_sib, spread_all, lines),
        in_specs=[spec_smem] + [spec_vmem] * 4,
    )
    att_far, w_out = tie((att_far, w_out))
    att = att_near, att_sib, att_far, send(att_far, 1)

    resid, x_two, comb, buffer = call(
        functools.partial(router_body, n_dp),
        (
            shaped((rows, width), F32),
            shaped((rows, width), BF16),
            shaped((rows, 128), F32),
            shaped((slots, wide + width), BF16),
        ),
        (
            *(place, tokens, cotangent, *att, w_out),
            *(w_in, vectors, routes, place_map),
        ),
        in_specs=[spec_smem] + [spec_vmem] * 11,
    )
    got = dispatch(buffer)

    back, grad_y, hidden, grad_pre = expert_call(place, got, (*own, *sib_own, *far))
    back_got = dispatch(back)

    rows_t, grad_y_t = call(turn_body, (shaped((width, slots), BF16),) * 2, (got, grad_y))
    sent = weight_grads(rows_t, grad_y_t, hidden, grad_pre, 3, BF16)
    rows_t, sent = tie((rows_t, sent))
    sibs = [send(array, 1) for array in sent]
    sent_own = weight_grads(rows_t, grad_y_t, hidden, grad_pre, 2, BF16)
    rows_t, sent_own = tie((rows_t, sent_own))
    sibs_own = [send(array, 1) for array in sent_own]
    away_sum = weight_grads(rows_t, grad_y_t, hidden, grad_pre, 1, BF16, sibs, True)
    far_sum = lax.all_gather(away_sum, "shard", axis_index_groups=pairs)
    back_got, rows_t = tie((back_got, rows_t))

    resid_grad, att_grad, dlogits, ln_two_sums = call(
        functools.partial(token_back_body, n_dp),
        (
            shaped((rows, width), F32),
            shaped((rows, width), BF16),
            shaped((rows, 128), BF16),
            shaped((8, width), F32),
        ),
        (back_got, cols, routes, comb, cotangent, resid, w_in, vectors),
    )
    grad_far = send(att_grad, 2)
    grad_sib = send(att_grad, 1)
    rows_t, grad_sib = tie((rows_t, grad_sib))
    own_new = weight_grads(rows_t, grad_y_t, hidden, grad_pre, 0, F32, sibs_own)
    layer_out, gate_part = call(
        functools.partial(layer_out_body, held, n_dp),
        (shaped((rows, width), BF16), shaped((padded, 128), F32)),
        (back_got, cols, comb, resid, x_two, dlogits, ln_two_sums),
    )
    grad_far, layer_out, own_new = tie((grad_far, layer_out, own_new))
    grad_last = send(grad_far, 1)
    extent = padded // n_shard
    head_grad, *out_pieces = call(
        functools.partial(projection_back_body, held),
        (shaped((group_len, part), BF16), *[shaped((extent, part), BF16)] * n_shard),
        (place, att_wide, w_out, att_grad, grad_sib, grad_far, grad_last),
        in_specs=[spec_smem] + [spec_vmem] * 6,
        scratch_shapes=[
            pltpu.VMEM((group_len, width), BF16),
            pltpu.VMEM((padded, part), BF16),
        ],
    )
    out_pieces = exchange(out_pieces)
    second_owned, *norm_part = call(
        functools.partial(attention_back_body, held),
        (shaped((padded, last_wide), BF16), *[shaped((rows, width), BF16)] * n_shard),
        (
            *(bounds, place, n_one, qkv, att_wide, log_total, w_in, gate_part, head_grad),
            normed_one,
        ),
        in_specs=[spec_smem] * 2 + [spec_vmem] * 8,
        scratch_shapes=[
            pltpu.VMEM((group_len, 3 * part), BF16),
            pltpu.VMEM((group_len, part), F32),
            pltpu.VMEM((group_len, part), F32),
        ],
    )
    near_sib = send(norm_part[1], 1)
    far_sib = send(norm_part[3], 1)
    norm_far = send((norm_part[2].astype(F32) + far_sib.astype(F32)).astype(BF16), 2)
    second_owned = call(
        assemble_body,
        shaped((padded, last_wide), BF16),
        (place, second_owned, *out_pieces),
        grid=(2,),
        in_specs=[spec_smem, pl.BlockSpec(memory_space=pl.ANY)]
        + [pl.BlockSpec((extent, part), lambda c: (0, 0))] * n_shard,
        out_specs=pl.BlockSpec((padded, 128), lambda c: (0, in_wide // 128 + c)),
        input_output_aliases={1: 0},
    )
    second_got = swap(second_owned.reshape(n_all, PAD, last_wide)).reshape(padded, last_wide)
    grads_new = new_grads_call(place, own_new, far_sum)
    norm_far, grads_new = tie((norm_far, grads_new))
    grad_tokens = call(
        first_norm_back_body,
        shaped((rows, width), BF16),
        (norm_part[0], near_sib, norm_far, tokens, vectors, resid_grad),
    )
    *grads_in, grad_out, grad_gate, ln_sums = call(
        functools.partial(second_sums_body, held, part, n_dp),
        (*[shaped((held, width), F32)] * 4, shaped((held, n_dp), F32), shaped((4, held), F32)),
        (second_got,),
    )
    return (
        *(layer_out, grad_tokens, *grads_in, grad_out),
        *(ln_sums[0], ln_sums[1], ln_sums[2], ln_sums[3]),
        *(grad_gate, *grads_new),
    )


def solution(mesh):
    flat = P(BOTH)
    lines = P(BOTH, None)
    in_specs = (
        (lines, P("dp", None), lines)
        + (flat, flat)
        + (lines,) * 4
        + (flat, flat, lines, lines)
        + (P("dp", None, "shard"), P("dp", "shard", None)) * 2
        + (lines,)
    )
    out_specs = (
        (lines,) * 6
        + (flat,) * 4
        + (lines, P("dp", None, "shard"), P("dp", "shard", None))
    )
    return jax.shard_map(
        per_device, mesh=mesh, in_specs=in_specs, out_specs=out_specs, check_vma=False
    )
```
